512 devices in a mesh: section: 16 (over y, core), tensor: 4 (over z_hi), seq: 8 (over z_lo, x).
Axes of the slice: x: 4, y: 8, z: 8 (z_hi: 4, z_lo: 2; z = z_hi * 2 + z_lo), core: 2. Of those that a mesh axis runs over, the one named last changes fastest.
Arguments:
- queries: bfloat16 [16, 2048, 4096], P('section', 'seq', 'tensor'), may hold values from -6 to 6
- keys: bfloat16 [16, 2048, 512], P('section', 'seq', 'tensor'), may hold values from -6 to 6
- values: bfloat16 [16, 2048, 512], P('section', 'seq', 'tensor'), may hold values from -6 to 6
- cotangent: bfloat16 [16, 2048, 4096], P('section', 'seq', 'tensor'), may hold values from -6 to 6
- positions: int32 [2048], replicated, may hold values from 0 to 2047, as said below
Outputs:
- attn_out: bfloat16 [16, 2048, 4096], P('section', 'seq', 'tensor')
- grad_q: bfloat16 [16, 2048, 4096], P('section', 'seq', 'tensor')
- grad_k: bfloat16 [16, 2048, 512], P('section', 'seq', 'tensor')
- grad_v: bfloat16 [16, 2048, 512], P('section', 'seq', 'tensor')
The draws below stay inside these ranges and needn't reach their ends.
Inputs may be any that keep to these rules, and one draw needn't show every extreme that they name: A permutation of 0 to 2047 in which every aligned block of 64 entries holds consecutive rising positions that start at a multiple of 64.
All inputs are finite; a program needn't handle non-finite values.
Results may differ from the reference program's by a relative error of at most 0.024.
Values may be sent and summed in bfloat16 or wider, within the bound.
A program may use at most 64 MiB of HBM per device.

```python
import jax
import jax.numpy as jnp
from jax import lax

HD = 128
HQ = 32
HK = 4
TOK_DEV = 256
SEQ = 2048
RUN = 64
SECTIONS = 16


def draw_queries(key, part):
    key = jax.random.fold_in(key, 11)
    shape = (SECTIONS, SEQ, HQ * HD)
    result = jnp.clip(jax.random.normal(key, shape, jnp.float32), -6.0, 6.0)
    return result.astype(jnp.bfloat16)


def draw_keys(key, part):
    key = jax.random.fold_in(key, 23)
    shape = (SECTIONS, SEQ, HK * HD)
    result = jnp.clip(jax.random.normal(key, shape, jnp.float32), -6.0, 6.0)
    return result.astype(jnp.bfloat16)


def draw_positions(key, part):
    key = jax.random.fold_in(key, 37)
    order = jax.random.permutation(key, SEQ // RUN)
    within = jnp.arange(RUN, dtype=jnp.int32)
    return (order.astype(jnp.int32)[:, None] * RUN + within[None, :]).reshape(SEQ).astype(jnp.int32)


def block_scale(key, dims, split, least, high):
    def one(axis_at, blocks):
        draws = jax.random.uniform(jax.random.fold_in(jax.random.fold_in(key, 6), axis_at), (blocks,), jnp.float32, least / len(split), high / len(split))
        return jnp.repeat(jnp.exp(draws), dims[axis_at] // blocks).reshape((-1,) + (1,) * (len(dims) - axis_at - 1))

    level = one(*split[0])
    for cut in split[1:]:
        level = level * one(*cut)
    return level


def centred(rng, dims, scale, reach, cuts=(), held_as=jnp.bfloat16):
    gain = block_scale(rng, dims, cuts, -0.22, 0.18) if cuts else 1.0
    entries = jax.random.normal(rng, dims, jnp.float32) * scale * gain
    return jnp.minimum(jnp.maximum(entries, -reach), reach).astype(held_as)


def setup_inputs(seed: int = 0) -> dict:
    key_list = jax.random.split(jax.random.key(seed), 6)
    return {
        "queries": draw_queries(jax.random.fold_in(key_list[5], 71), 0),
        "keys": draw_keys(jax.random.fold_in(key_list[5], 71), 0),
        "values": centred(key_list[2], (SECTIONS, SEQ, HK * HD), 1.0, 6.0, ((0, 16), (1, 8), (2, 4))),
        "cotangent": centred(key_list[3], (SECTIONS, SEQ, HQ * HD), 1.0, 6.0, ((0, 16), (1, 8), (2, 4))),
        "positions": draw_positions(jax.random.fold_in(key_list[5], 71), 0),
    }


def round_bf(x):
    return lax.optimization_barrier(x.astype(jnp.bfloat16)).astype(jnp.float32)


def shard_pass(q_rows, cot_rows, q_pos, keys_all, values_all, positions):
    group = HQ // HK
    scale = HD ** -0.5
    qh = q_rows.reshape(TOK_DEV, HK, group, HD).astype(jnp.float32)
    doh = cot_rows.reshape(TOK_DEV, HK, group, HD).astype(jnp.float32)
    kh = keys_all.reshape(SEQ, HK, HD).astype(jnp.float32)
    vh = values_all.reshape(SEQ, HK, HD).astype(jnp.float32)
    visible = positions[None, :] <= q_pos[:, None]
    scores = jnp.einsum("tkgd,skd->kgts", qh, kh) * scale
    scores = jnp.where(visible, scores, -1e30)
    top = jnp.max(scores, axis=-1)
    lse = top + jnp.log(jnp.sum(jnp.exp(scores - top[..., None]), axis=-1))
    probs = jnp.where(visible, jnp.exp(scores - lse[..., None]), 0.0)
    probs_b = round_bf(probs)
    out = jnp.einsum("kgts,skd->tkgd", probs_b, vh).astype(jnp.bfloat16)
    dvec = jnp.einsum("tkgd,tkgd->kgt", doh, out.astype(jnp.float32))
    dprobs = jnp.einsum("tkgd,skd->kgts", doh, vh)
    dscores = round_bf(probs * (dprobs - dvec[..., None]))
    grad_q = (jnp.einsum("kgts,skd->tkgd", dscores, kh) * scale).astype(jnp.bfloat16)
    part_k = (jnp.einsum("kgts,tkgd->skd", dscores, qh) * scale).astype(jnp.bfloat16)
    part_v = jnp.einsum("kgts,tkgd->skd", probs_b, doh).astype(jnp.bfloat16)
    return out.reshape(TOK_DEV, HQ * HD), grad_q.reshape(TOK_DEV, HQ * HD), part_k.reshape(SEQ, HK * HD), part_v.reshape(SEQ, HK * HD)


def section_pass(items, positions):
    q_all, k_all, v_all, cot_all = items

    def one_block(index):
        start = (index * TOK_DEV).astype(jnp.int32)
        q_rows = lax.dynamic_slice_in_dim(q_all, start, TOK_DEV, 0)
        cot_rows = lax.dynamic_slice_in_dim(cot_all, start, TOK_DEV, 0)
        q_pos = lax.dynamic_slice_in_dim(positions, start, TOK_DEV, 0)
        return shard_pass(q_rows, cot_rows, q_pos, k_all, v_all, positions)

    out, grad_q, part_k, part_v = lax.map(one_block, jnp.arange(SEQ // TOK_DEV, dtype=jnp.int32))
    grad_k = jnp.sum(part_k.astype(jnp.float32), axis=0).astype(jnp.bfloat16)
    grad_v = jnp.sum(part_v.astype(jnp.float32), axis=0).astype(jnp.bfloat16)
    return out.reshape(SEQ, HQ * HD), grad_q.reshape(SEQ, HQ * HD), grad_k, grad_v


def reference(queries, keys, values, cotangent, positions):
    cot_layer = cotangent[::-1]
    return lax.map(lambda items: section_pass(items, positions), (queries, keys, values, cot_layer))
```

```python
import functools
import math

import jax
import jax.numpy as jnp
from jax import lax
from jax.experimental import pallas as pl
from jax.experimental.pallas import tpu as pltpu
from jax.sharding import PartitionSpec as P

HD = 128
MESH = pl.DeviceIdType.MESH
NT = (((1,), (1,)), ((), ()))
NN = (((1,), (0,)), ((), ()))
F32 = jnp.float32
BF16 = jnp.bfloat16


def dot(a, b, dims):
    return lax.dot_general(a, b, dims, preferred_element_type=F32)


def peers():
    section, tensor, seq = (lax.axis_index(a) for a in ("section", "tensor", "seq"))
    z, x = seq // 4, seq % 4
    found = []
    for slot in range(1, 8):
        dz, dx = slot // 4, slot % 4
        there = ((z + dz) % 2) * 4 + (x + dx) % 4
        back = dz * 4 + (4 - dx) % 4
        found.append((slot, back, (section, tensor, there)))
    return found


def greet(others):
    barrier = pltpu.get_barrier_semaphore()
    for _, _, device in others:
        pl.semaphore_signal(barrier, inc=1, device_id=device, device_id_type=MESH)
    pl.semaphore_wait(barrier, len(others))


def remote(src, dst, send, recv, device):
    return pltpu.make_async_remote_copy(
        src_ref=src, dst_ref=dst, send_sem=send, recv_sem=recv, device_id=device, device_id_type=MESH
    )


def fwd_kernel(
    heads, tok, q_hbm, k_hbm, v_hbm, pos_ref, o_ref, p_hbm, k_out, v_out, stat_ref,
    qst, kbuf, vbuf, scores, probs, otr, bias, top, total, qsem, ksend, krecv, vsend, vrecv, osem, psem,
):
    others = peers()
    loads = []
    for h in range(heads):
        loads.append(
            pltpu.make_async_copy(
                q_hbm.at[:, pl.ds(h * HD, HD)], qst.at[pl.ds(h * tok, tok), :], qsem.at[h]
            )
        )
    loads.append(pltpu.make_async_copy(k_hbm, kbuf.at[0], qsem.at[heads]))
    loads.append(pltpu.make_async_copy(v_hbm, vbuf.at[0], qsem.at[heads + 1]))
    for c in loads:
        c.start()
    greet(others)
    sends = []
    for slot, back, device in others:
        sends.append(remote(k_hbm, kbuf.at[back], ksend.at[slot], krecv.at[back], device))
    for slot, back, device in others:
        sends.append(remote(v_hbm, vbuf.at[back], vsend.at[slot], vrecv.at[back], device))
    for c in sends:
        c.start()
    for c in loads:
        c.wait()

    seq = lax.axis_index("seq")
    z, x = seq // 4, seq % 4
    q_row = pos_ref[pl.ds(seq, 1), :]
    rows = [
        pos_ref[pl.ds(((z + slot // 4) % 2) * 4 + (x + slot % 4) % 4, 1), :] for slot in range(8)
    ]
    k_cols = jnp.transpose(jnp.concatenate(rows, axis=0))
    for slot in range(8):
        visible = k_cols[:, slot : slot + 1] <= q_row
        bias[slot] = jnp.where(visible, 0.0, -1e30)
    top[...] = jnp.full_like(top, -1e30)
    total[...] = jnp.zeros_like(total)
    factor = HD**-0.5 * math.log2(math.e)

    def score(slot):
        kb = kbuf[slot]
        bb = bias[slot]
        for h in range(heads):
            part = dot(kb, qst[h * tok : (h + 1) * tok, :], NT) * factor + bb
            scores[slot, :, h * tok : (h + 1) * tok] = part
            top[h] = jnp.maximum(top[h], jnp.max(part.reshape(tok // 8, 8, tok), axis=0))

    score(0)

    def score_step(slot, carry):
        remote(kbuf.at[slot], kbuf.at[slot], ksend.at[slot], krecv.at[slot], others[0][2]).wait_recv()
        score(slot)
        return carry

    lax.fori_loop(1, 8, score_step, 0)
    for h in range(heads):
        top[h] = jnp.broadcast_to(jnp.max(top[h], axis=0, keepdims=True), (8, tok))

    otr[...] = jnp.zeros_like(otr)

    def mix(slot):
        vt = jnp.transpose(vbuf[slot])
        for h in range(heads):
            columns = slice(h * tok, (h + 1) * tok)
            raw = jnp.exp2(scores[slot, :, columns] - top[h, 0:1, :])
            total[h] += jnp.sum(raw.reshape(tok // 8, 8, tok), axis=0)
            pb = raw.astype(BF16)
            probs[slot, :, columns] = pb
            otr[:, columns] += dot(vt, pb, NN)
        pltpu.make_async_copy(probs.at[slot], p_hbm.at[slot], psem.at[slot]).start()

    mix(0)

    def mix_step(slot, carry):
        remote(vbuf.at[slot], vbuf.at[slot], vsend.at[slot], vrecv.at[slot], others[0][2]).wait_recv()
        mix(slot)
        return carry

    lax.fori_loop(1, 8, mix_step, 0)

    outs = [
        pltpu.make_async_copy(kbuf, k_out, osem.at[0]),
        pltpu.make_async_copy(vbuf, v_out, osem.at[1]),
    ]
    for c in outs:
        c.start()
    inverse = []
    for h in range(heads):
        columns = slice(h * tok, (h + 1) * tok)
        inv = 1.0 / jnp.sum(total[h], axis=0, keepdims=True)
        inverse.append(inv)
        o_ref[:, h * HD : (h + 1) * HD] = jnp.transpose(otr[:, columns] * inv).astype(BF16)
    stat_ref[...] = jnp.transpose(jnp.concatenate(inverse, axis=0))
    for c in sends:
        c.wait_send()
    for c in outs:
        c.wait()
    for slot in range(8):
        pltpu.make_async_copy(probs.at[slot], p_hbm.at[slot], psem.at[slot]).wait()


def bwd_kernel(
    heads, tok, q_hbm, cot_hbm, p_hbm, k_hbm, v_hbm, o_ref, stat_ref, gq_ref, gk_ref, gv_ref,
    qst, cst, probs, kbuf, vbuf, dst, dqt, sendbuf, recvbuf, own, qsem, psem, ksem, ssem, rsem,
):
    others = peers()
    scale = HD**-0.5
    loads = []
    for h in range(heads):
        loads.append(
            pltpu.make_async_copy(
                cot_hbm.at[:, pl.ds(h * HD, HD)], cst.at[pl.ds(h * tok, tok), :], qsem.at[h]
            )
        )
        loads.append(
            pltpu.make_async_copy(
                q_hbm.at[:, pl.ds(h * HD, HD)], qst.at[pl.ds(h * tok, tok), :], qsem.at[heads + h]
            )
        )
    loads.append(pltpu.make_async_copy(k_hbm, kbuf, ksem.at[0]))
    loads.append(pltpu.make_async_copy(v_hbm, vbuf, ksem.at[1]))
    for c in loads:
        c.start()
    for slot in range(8):
        pltpu.make_async_copy(p_hbm.at[slot], probs.at[slot], psem.at[slot]).start()
    greet(others)
    for c in loads:
        c.wait()

    columns = []
    for h in range(heads):
        rows = slice(h * tok, (h + 1) * tok)
        inv = stat_ref[:, h : h + 1]
        cot = cst[rows, :].astype(F32)
        columns.append(
            jnp.sum(cot * o_ref[:, h * HD : (h + 1) * HD].astype(F32), axis=1, keepdims=True) * inv
        )
        cst[rows, :] = (cot * inv).astype(BF16)
    dvec = jnp.transpose(jnp.concatenate(columns, axis=1))
    dqt[...] = jnp.zeros_like(dqt)

    def work(slot):
        pltpu.make_async_copy(p_hbm.at[slot], probs.at[slot], psem.at[slot]).wait()
        vb = vbuf[slot]
        kt = jnp.transpose(kbuf[slot])
        for h in range(heads):
            rows = slice(h * tok, (h + 1) * tok)
            dp = dot(vb, cst[rows, :], NT)
            ds = (probs[slot, :, rows].astype(F32) * (dp - dvec[h : h + 1, :])).astype(BF16)
            dst[:, rows] = ds
            dqt[:, rows] += dot(kt, ds, NN)
        dk = dot(dst[...], qst[...], NN) * scale
        dv = dot(probs[slot], cst[...], NN)
        return dk, dv

    def step(slot, carry):
        dk, dv = work(slot)
        sendbuf[slot, 0] = dk.astype(BF16)
        sendbuf[slot, 1] = dv.astype(BF16)
        dz, dx = slot // 4, slot % 4
        section, tensor, seq = (lax.axis_index(a) for a in ("section", "tensor", "seq"))
        z, x = seq // 4, seq % 4
        there = ((z + dz) % 2) * 4 + (x + dx) % 4
        back = dz * 4 + (4 - dx) % 4
        remote(
            sendbuf.at[slot], recvbuf.at[back], ssem.at[slot], rsem.at[back], (section, tensor, there)
        ).start()
        return carry

    lax.fori_loop(1, 8, step, 0)
    dk, dv = work(0)
    own[0] = dk
    own[1] = dv
    for h in range(heads):
        part = dqt[:, h * tok : (h + 1) * tok] * scale
        gq_ref[:, h * HD : (h + 1) * HD] = jnp.transpose(part).astype(BF16)
    for slot, back, device in others:
        remote(sendbuf.at[slot], recvbuf.at[slot], ssem.at[slot], rsem.at[slot], device).wait()
        own[0] += recvbuf[slot, 0].astype(F32)
        own[1] += recvbuf[slot, 1].astype(F32)
    gk_ref[...] = own[0].astype(BF16)
    gv_ref[...] = own[1].astype(BF16)


def local(queries, keys, values, cotangent, positions):
    q, k, v, cot = queries[0], keys[0], values[0], cotangent[0]
    tok, width = q.shape
    heads = width // HD
    wide = heads * tok
    count = lax.axis_size("section")
    mirrored = lax.ppermute(cot, "section", [(s, count - 1 - s) for s in range(count)])
    pos = positions.reshape(8, tok).astype(F32)
    anywhere = pl.BlockSpec(memory_space=pl.ANY)
    vmem = pl.BlockSpec(memory_space=pltpu.VMEM)
    dma = pltpu.SemaphoreType.DMA
    out, probs, k_all, v_all, stat = pl.pallas_call(
        functools.partial(fwd_kernel, heads, tok),
        out_shape=(
            jax.ShapeDtypeStruct((tok, width), BF16),
            jax.ShapeDtypeStruct((8, tok, wide), BF16),
            jax.ShapeDtypeStruct((8, tok, HD), BF16),
            jax.ShapeDtypeStruct((8, tok, HD), BF16),
            jax.ShapeDtypeStruct((tok, heads), F32),
        ),
        in_specs=[anywhere, anywhere, anywhere, vmem],
        out_specs=(vmem, anywhere, anywhere, anywhere, vmem),
        scratch_shapes=[
            pltpu.VMEM((wide, HD), BF16),
            pltpu.VMEM((8, tok, HD), BF16),
            pltpu.VMEM((8, tok, HD), BF16),
            pltpu.VMEM((8, tok, wide), F32),
            pltpu.VMEM((8, tok, wide), BF16),
            pltpu.VMEM((HD, wide), F32),
            pltpu.VMEM((8, tok, tok), F32),
            pltpu.VMEM((heads, 8, tok), F32),
            pltpu.VMEM((heads, 8, tok), F32),
            dma((heads + 2,)),
            dma((8,)),
            dma((8,)),
            dma((8,)),
            dma((8,)),
            dma((2,)),
            dma((8,)),
        ],
        cost_estimate=pl.CostEstimate(
            flops=4 * wide * 8 * tok * HD, bytes_accessed=2**24, transcendentals=wide * 8 * tok
        ),
        compiler_params=pltpu.CompilerParams(
            collective_id=1, has_side_effects=True, vmem_limit_bytes=48 * 2**20
        ),
    )(q, k, v, pos)
    grad_q, grad_k, grad_v = pl.pallas_call(
        functools.partial(bwd_kernel, heads, tok),
        out_shape=(
            jax.ShapeDtypeStruct((tok, width), BF16),
            jax.ShapeDtypeStruct((tok, HD), BF16),
            jax.ShapeDtypeStruct((tok, HD), BF16),
        ),
        in_specs=[anywhere] * 5 + [vmem] * 2,
        out_specs=(vmem, vmem, vmem),
        scratch_shapes=[
            pltpu.VMEM((wide, HD), BF16),
            pltpu.VMEM((wide, HD), BF16),
            pltpu.VMEM((8, tok, wide), BF16),
            pltpu.VMEM((8, tok, HD), BF16),
            pltpu.VMEM((8, tok, HD), BF16),
            pltpu.VMEM((tok, wide), BF16),
            pltpu.VMEM((HD, wide), F32),
            pltpu.VMEM((8, 2, tok, HD), BF16),
            pltpu.VMEM((8, 2, tok, HD), BF16),
            pltpu.VMEM((2, tok, HD), F32),
            dma((2 * heads,)),
            dma((8,)),
            dma((2,)),
            dma((8,)),
            dma((8,)),
        ],
        cost_estimate=pl.CostEstimate(
            flops=8 * wide * 8 * tok * HD, bytes_accessed=2**24, transcendentals=0
        ),
        compiler_params=pltpu.CompilerParams(
            collective_id=2, has_side_effects=True, vmem_limit_bytes=48 * 2**20
        ),
    )(q, mirrored, probs, k_all, v_all, out, stat)
    return (out[None], grad_q[None], grad_k[None], grad_v[None])


def solution(mesh):
    split = P("section", "seq", "tensor")
    return jax.shard_map(
        local,
        mesh=mesh,
        in_specs=(split, split, split, split, P()),
        out_specs=(split, split, split, split),
        check_vma=False,
    )
```

```python
import functools
import math

import jax
import jax.numpy as jnp
from jax import lax
from jax.experimental import pallas as pl
from jax.experimental.pallas import tpu as pltpu
from jax.sharding import PartitionSpec as P

HD = 128
MESH = pl.DeviceIdType.MESH
NT = (((1,), (1,)), ((), ()))
NN = (((1,), (0,)), ((), ()))
F32 = jnp.float32
BF16 = jnp.bfloat16
UNROLL = 8
SPREAD = 8
WEIGH = 1


def dot(a, b, dims):
    return lax.dot_general(a, b, dims, preferred_element_type=F32)


def place():
    return tuple(lax.axis_index(a) for a in ("section", "tensor", "seq"))


ORDER = ((1, 2), (0, 2), (1, 1), (1, 3), (0, 1), (0, 3), (1, 0), (0, 0))
OWN = 7


def peer(dz, dx):
    section, tensor, seq = place()
    z, x = seq // 4, seq % 4
    return (section, tensor, ((z + dz) % 2) * 4 + (x + dx) % 4)


def greet(devices):
    barrier = pltpu.get_barrier_semaphore()
    for device in devices:
        pl.semaphore_signal(barrier, inc=1, device_id=device, device_id_type=MESH)
    pl.semaphore_wait(barrier, len(devices))


def remote(src, dst, send, recv, device):
    return pltpu.make_async_remote_copy(
        src_ref=src, dst_ref=dst, send_sem=send, recv_sem=recv, device_id=device, device_id_type=MESH
    )


def each(count, body, unroll=1):
    if unroll >= count:
        for j in range(count):
            body(j)
        return

    def step(i, carry):
        for j in range(unroll):
            body(i * unroll + j)
        return carry

    lax.fori_loop(0, count // unroll, step, 0)


def block(index, size):
    return pl.ds(index * size if isinstance(index, int) else pl.multiple_of(index * size, size), size)


def fwd_kernel(
    heads, tok, q_hbm, k_hbm, v_hbm, pos_hbm, o_ref, probs, kbuf, vbuf, qst, inv_ref,
    pos, scores, bias, top, total, lsem, ksend, krecv, vsend, vrecv,
):
    loads = [
        pltpu.make_async_copy(q_hbm.at[:, pl.ds(h * HD, HD)], qst.at[pl.ds(h * tok, tok), :], lsem.at[h])
        for h in range(heads)
    ]
    loads.append(pltpu.make_async_copy(k_hbm, kbuf.at[OWN], lsem.at[heads]))
    loads.append(pltpu.make_async_copy(v_hbm, vbuf.at[OWN], lsem.at[heads + 1]))
    loads.append(pltpu.make_async_copy(pos_hbm, pos, lsem.at[heads + 2]))
    for c in loads:
        c.start()
    greet([peer(*ORDER[slot]) for slot in range(OWN)])
    sends = []
    for src, buf, send, recv in ((k_hbm, kbuf, ksend, krecv), (v_hbm, vbuf, vsend, vrecv)):
        for slot in range(OWN):
            dz, dx = ORDER[slot]
            back = ORDER.index((dz, (4 - dx) % 4))
            sends.append(remote(src, buf.at[back], send.at[slot], recv.at[back], peer(dz, dx)))
    for c in sends:
        c.start()
    for c in loads:
        c.wait()

    def pos_row(device):
        return pos[block(device, tok)].reshape(1, tok).astype(F32)

    rows = [pos_row(peer(dz, dx)[2]) for dz, dx in ORDER]
    k_cols = jnp.transpose(jnp.concatenate(rows, axis=0))
    for slot in range(8):
        bias[slot] = jnp.where(k_cols[:, slot : slot + 1] <= rows[OWN], 0.0, -1e30)
    top[...] = jnp.full_like(top, -1e30)
    total[...] = jnp.zeros_like(total)
    factor = HD**-0.5 * math.log2(math.e)

    def score(i):
        slot = OWN - i

        @pl.when(i > 0)
        def _():
            remote(kbuf.at[slot], kbuf.at[slot], ksend.at[slot], krecv.at[slot], peer(0, 1)).wait_recv()

        def one(h):
            columns = block(h, tok)
            part = dot(kbuf[slot], qst[columns, :], NT) * factor + bias[slot]
            scores[slot, :, columns] = part
            top[h] = jnp.maximum(top[h], jnp.max(part.reshape(tok // 8, 8, tok), axis=0))

        each(heads, one, UNROLL)

    each(8, score)

    def weigh(h):
        columns = block(h, tok)
        peak = jnp.max(top[h], axis=0, keepdims=True)

        def one(slot):
            raw = jnp.exp2(scores[slot, :, columns] - peak)
            total[h] += jnp.sum(raw.reshape(tok // 8, 8, tok), axis=0)
            probs[slot, :, columns] = raw.astype(BF16)

        each(8, one, UNROLL)

    each(heads, weigh, WEIGH)
    for slot in range(OWN):
        remote(vbuf.at[slot], vbuf.at[slot], vsend.at[slot], vrecv.at[slot], peer(0, 1)).wait_recv()
    vt = jnp.transpose(vbuf[...].reshape(8 * tok, HD))

    def mix(h):
        inv = jnp.broadcast_to(1.0 / jnp.sum(total[h], axis=0, keepdims=True), (HD, tok))
        mixed = dot(vt, probs[:, :, block(h, tok)].reshape(8 * tok, tok), NN)
        o_ref[:, block(h, HD)] = jnp.transpose(mixed * inv).astype(BF16)
        inv_ref[:, block(h, HD)] = jnp.transpose(inv)

    each(heads, mix, SPREAD)
    for c in sends:
        c.wait_send()


def bwd_kernel(
    heads, tok, cot_ref, probs, kbuf, vbuf, qst, o_ref, inv_ref, gq_ref, gk_ref, gv_ref,
    cst, dst, acc, dvec, sendbuf, far, near, across, ssem, rsem,
):
    scale = HD**-0.5
    right, left, over = peer(0, 1), peer(0, 3), peer(1, 0)
    greet([right, left, over])

    def prepare(h):
        columns = block(h, HD)
        cot = cot_ref[:, columns].astype(F32) * inv_ref[:, columns]
        drop = jnp.transpose(cot * o_ref[:, columns].astype(F32))
        dvec[pl.ds(h, 1), :] = jnp.sum(drop, axis=0, keepdims=True)
        cst[block(h, tok), :] = cot.astype(BF16)

    each(heads, prepare, SPREAD)

    def far_k(dz):
        return remote(sendbuf.at[1 - dz, 0], far.at[dz, 0], ssem.at[dz], rsem.at[dz], right)

    def far_v(dz):
        return remote(sendbuf.at[1 - dz, 1], far.at[dz, 1], ssem.at[2 + dz], rsem.at[2 + dz], left)

    def near_right(dz):
        return remote(sendbuf.at[4 - 2 * dz], near.at[dz, 0], ssem.at[4 + dz], rsem.at[4 + dz], right)

    def near_left(dz):
        return remote(sendbuf.at[5 - 2 * dz], near.at[dz, 1], ssem.at[6 + dz], rsem.at[6 + dz], left)

    def work(slot):
        def one(h):
            rows = block(h, tok)
            dp = dot(vbuf[slot], cst[rows, :], NT)
            part = probs[slot, :, rows].astype(F32) * (dp - dvec[pl.ds(h, 1), :])
            dst[slot, :, rows] = part.astype(BF16)

        each(heads, one, UNROLL)
        acc[0] = dot(dst[slot], qst[...], NN) * scale
        acc[1] = dot(probs[slot], cst[...], NN)

        @pl.when(slot < 2)
        def _():
            sendbuf[slot] = acc[0:2].astype(BF16)
            far_k(1 - slot).start()
            far_v(1 - slot).start()

        for dz in range(2):

            @pl.when(slot == 4 - 2 * dz)
            def _():
                far_k(dz).wait_recv()
                sendbuf[slot, 0] = (acc[0] + far[dz, 0].astype(F32)).astype(BF16)
                sendbuf[slot, 1] = acc[1].astype(BF16)
                near_right(dz).start()

            @pl.when(slot == 5 - 2 * dz)
            def _():
                far_v(dz).wait_recv()
                sendbuf[slot, 0] = acc[0].astype(BF16)
                sendbuf[slot, 1] = (acc[1] + far[dz, 1].astype(F32)).astype(BF16)
                near_left(dz).start()

        @pl.when(slot == 6)
        def _():
            acc[2:4] = acc[0:2]

    each(8, work)

    near_right(1).wait_recv()
    near_left(1).wait_recv()
    sendbuf[6] = (acc[2:4] + near[1, 0].astype(F32) + near[1, 1].astype(F32)).astype(BF16)
    cross = remote(sendbuf.at[6], across, ssem.at[8], rsem.at[8], over)
    cross.start()
    kt = jnp.transpose(kbuf[...].reshape(8 * tok, HD))

    def finish(h):
        part = dot(kt, dst[:, :, block(h, tok)].reshape(8 * tok, tok), NN) * scale
        gq_ref[:, block(h, HD)] = jnp.transpose(part).astype(BF16)

    each(heads, finish, SPREAD)
    near_right(0).wait_recv()
    near_left(0).wait_recv()
    cross.wait_recv()
    summed = acc[0:2] + near[0, 0].astype(F32) + near[0, 1].astype(F32) + across[...].astype(F32)
    gk_ref[...] = summed[0].astype(BF16)
    gv_ref[...] = summed[1].astype(BF16)
    cross.wait_send()
    for dz in range(2):
        for make in (far_k, far_v, near_right, near_left):
            make(dz).wait_send()


def local(queries, keys, values, cotangent, positions):
    q, k, v, cot = queries[0], keys[0], values[0], cotangent[0]
    tok, width = q.shape
    heads = width // HD
    wide = heads * tok
    count = lax.axis_size("section")
    mirrored = lax.ppermute(cot, "section", [(s, count - 1 - s) for s in range(count)])
    anywhere = pl.BlockSpec(memory_space=pl.ANY)
    vmem = pl.BlockSpec(memory_space=pltpu.VMEM)
    dma = pltpu.SemaphoreType.DMA
    out, probs, k_all, v_all, q_st, inverse = pl.pallas_call(
        functools.partial(fwd_kernel, heads, tok),
        out_shape=(
            jax.ShapeDtypeStruct((tok, width), BF16),
            jax.ShapeDtypeStruct((8, tok, wide), BF16),
            jax.ShapeDtypeStruct((8, tok, HD), BF16),
            jax.ShapeDtypeStruct((8, tok, HD), BF16),
            jax.ShapeDtypeStruct((wide, HD), BF16),
            jax.ShapeDtypeStruct((tok, width), F32),
        ),
        in_specs=[anywhere] * 4,
        out_specs=(vmem,) * 6,
        scratch_shapes=[
            pltpu.VMEM((8 * tok,), jnp.int32),
            pltpu.VMEM((8, tok, wide), F32),
            pltpu.VMEM((8, tok, tok), F32),
            pltpu.VMEM((heads, 8, tok), F32),
            pltpu.VMEM((heads, 8, tok), F32),
            dma((heads + 3,)),
            dma((8,)),
            dma((8,)),
            dma((8,)),
            dma((8,)),
        ],
        cost_estimate=pl.CostEstimate(
            flops=4 * wide * 8 * tok * HD, bytes_accessed=2**24, transcendentals=wide * 8 * tok
        ),
        compiler_params=pltpu.CompilerParams(
            collective_id=1, has_side_effects=True, vmem_limit_bytes=36 * 2**20
        ),
    )(q, k, v, positions)
    grad_q, grad_k, grad_v = pl.pallas_call(
        functools.partial(bwd_kernel, heads, tok),
        out_shape=(
            jax.ShapeDtypeStruct((tok, width), BF16),
            jax.ShapeDtypeStruct((tok, HD), BF16),
            jax.ShapeDtypeStruct((tok, HD), BF16),
        ),
        in_specs=[vmem] * 7,
        out_specs=(vmem,) * 3,
        scratch_shapes=[
            pltpu.VMEM((wide, HD), BF16),
            pltpu.VMEM((8, tok, wide), BF16),
            pltpu.VMEM((4, tok, HD), F32),
            pltpu.VMEM((heads, tok), F32),
            pltpu.VMEM((7, 2, tok, HD), BF16),
            pltpu.VMEM((2, 2, tok, HD), BF16),
            pltpu.VMEM((2, 2, 2, tok, HD), BF16),
            pltpu.VMEM((2, tok, HD), BF16),
            dma((9,)),
            dma((9,)),
        ],
        cost_estimate=pl.CostEstimate(
            flops=8 * wide * 8 * tok * HD, bytes_accessed=2**24, transcendentals=0
        ),
        compiler_params=pltpu.CompilerParams(
            collective_id=2, has_side_effects=True, vmem_limit_bytes=36 * 2**20
        ),
    )(mirrored, probs, k_all, v_all, q_st, out, inverse)
    return (out[None], grad_q[None], grad_k[None], grad_v[None])


def solution(mesh):
    split = P("section", "seq", "tensor")
    return jax.shard_map(
        local,
        mesh=mesh,
        in_specs=(split, split, split, split, P()),
        out_specs=(split, split, split, split),
        check_vma=False,
    )
```

```python
import functools
import math

import jax
import jax.numpy as jnp
from jax import lax
from jax.experimental import pallas as pl
from jax.experimental.pallas import tpu as pltpu
from jax.sharding import PartitionSpec as P

HD = 128
MESH = pl.DeviceIdType.MESH
NT = (((1,), (1,)), ((), ()))
NN = (((1,), (0,)), ((), ()))
F32 = jnp.float32
BF16 = jnp.bfloat16
UNROLL = 8
SPREAD = 8
WEIGH = 1


def dot(a, b, dims):
    return lax.dot_general(a, b, dims, preferred_element_type=F32)


def place():
    return tuple(lax.axis_index(a) for a in ("section", "tensor", "seq"))


ORDER = ((1, 2), (1, 1), (1, 3), (0, 2), (1, 0), (0, 1), (0, 3), (0, 0))
OWN = 7


def peer(dz, dx):
    section, tensor, seq = place()
    z, x = seq // 4, seq % 4
    return (section, tensor, ((z + dz) % 2) * 4 + (x + dx) % 4)


def greet(devices):
    barrier = pltpu.get_barrier_semaphore()
    for device in devices:
        pl.semaphore_signal(barrier, inc=1, device_id=device, device_id_type=MESH)
    pl.semaphore_wait(barrier, len(devices))


def remote(src, dst, send, recv, device):
    return pltpu.make_async_remote_copy(
        src_ref=src, dst_ref=dst, send_sem=send, recv_sem=recv, device_id=device, device_id_type=MESH
    )


def each(count, body, unroll=1):
    if unroll >= count:
        for j in range(count):
            body(j)
        return

    def step(i, carry):
        for j in range(unroll):
            body(i * unroll + j)
        return carry

    lax.fori_loop(0, count // unroll, step, 0)


def block(index, size):
    return pl.ds(index * size if isinstance(index, int) else pl.multiple_of(index * size, size), size)


def fwd_kernel(
    heads, tok, q_hbm, k_hbm, v_hbm, pos_hbm, o_ref, probs, kbuf, vbuf, qst, inv_ref,
    pos, scores, bias, top, total, lsem, ksend, krecv, vsend, vrecv,
):
    loads = [
        pltpu.make_async_copy(q_hbm.at[:, pl.ds(h * HD, HD)], qst.at[pl.ds(h * tok, tok), :], lsem.at[h])
        for h in range(heads)
    ]
    loads.append(pltpu.make_async_copy(k_hbm, kbuf.at[OWN], lsem.at[heads]))
    loads.append(pltpu.make_async_copy(v_hbm, vbuf.at[OWN], lsem.at[heads + 1]))
    loads.append(pltpu.make_async_copy(pos_hbm, pos, lsem.at[heads + 2]))
    for c in loads:
        c.start()
    greet([peer(*ORDER[slot]) for slot in range(OWN)])
    sends = []
    for src, buf, send, recv in ((k_hbm, kbuf, ksend, krecv), (v_hbm, vbuf, vsend, vrecv)):
        for slot in range(OWN):
            dz, dx = ORDER[slot]
            back = ORDER.index((dz, (4 - dx) % 4))
            sends.append(remote(src, buf.at[back], send.at[slot], recv.at[back], peer(dz, dx)))
    for c in sends:
        c.start()
    for c in loads:
        c.wait()

    def pos_row(device):
        return pos[block(device, tok)].reshape(1, tok).astype(F32)

    rows = [pos_row(peer(dz, dx)[2]) for dz, dx in ORDER]
    k_cols = jnp.transpose(jnp.concatenate(rows, axis=0))
    for slot in range(8):
        bias[slot] = jnp.where(k_cols[:, slot : slot + 1] <= rows[OWN], 0.0, -1e30)
    top[...] = jnp.full_like(top, -1e30)
    total[...] = jnp.zeros_like(total)
    factor = HD**-0.5 * math.log2(math.e)

    def score(i):
        slot = OWN - i

        @pl.when(i > 0)
        def _():
            remote(kbuf.at[slot], kbuf.at[slot], ksend.at[slot], krecv.at[slot], peer(0, 1)).wait_recv()

        def one(h):
            columns = block(h, tok)
            part = dot(kbuf[slot], qst[columns, :], NT) * factor + bias[slot]
            scores[slot, :, columns] = part
            top[h] = jnp.maximum(top[h], jnp.max(part.reshape(tok // 8, 8, tok), axis=0))

        each(heads, one, UNROLL)

    each(8, score)

    def weigh(h):
        columns = block(h, tok)
        peak = jnp.max(top[h], axis=0, keepdims=True)

        def one(slot):
            raw = jnp.exp2(scores[slot, :, columns] - peak)
            total[h] += jnp.sum(raw.reshape(tok // 8, 8, tok), axis=0)
            probs[slot, :, columns] = raw.astype(BF16)

        each(8, one, UNROLL)

    each(heads, weigh, WEIGH)
    for slot in range(OWN):
        remote(vbuf.at[slot], vbuf.at[slot], vsend.at[slot], vrecv.at[slot], peer(0, 1)).wait_recv()
    vt = jnp.transpose(vbuf[...].reshape(8 * tok, HD))

    def mix(h):
        inv = jnp.broadcast_to(1.0 / jnp.sum(total[h], axis=0, keepdims=True), (HD, tok))
        mixed = dot(vt, probs[:, :, block(h, tok)].reshape(8 * tok, tok), NN)
        o_ref[:, block(h, HD)] = jnp.transpose(mixed * inv).astype(BF16)
        inv_ref[:, block(h, HD)] = jnp.transpose(inv)

    each(heads, mix, SPREAD)
    for c in sends:
        c.wait_send()


def bwd_kernel(
    heads, tok, cot_ref, probs, kbuf, vbuf, qst, o_ref, inv_ref, gq_ref, gk_ref, gv_ref,
    cst, dst, acc, hold, dvec, sendbuf, zin, far1, far0, near1, near0, across, ssem, rsem,
):
    scale = HD**-0.5
    right, left, over = peer(0, 1), peer(0, 3), peer(1, 0)
    greet([right, left, over])

    def prepare(h):
        columns = block(h, HD)
        cot = cot_ref[:, columns].astype(F32) * inv_ref[:, columns]
        drop = jnp.transpose(cot * o_ref[:, columns].astype(F32))
        dvec[pl.ds(h, 1), :] = jnp.sum(drop, axis=0, keepdims=True)
        cst[block(h, tok), :] = cot.astype(BF16)

    each(heads, prepare, SPREAD)

    def hop(number, src, dst_ref, device):
        return remote(src, dst_ref, ssem.at[number], rsem.at[number], device)

    top, low = pl.ds(0, tok // 2), pl.ds(tok // 2, tok // 2)
    pair = {dx: hop(dx, sendbuf.at[ORDER.index((1, dx)), 1], zin.at[dx], over) for dx in range(4)}
    far1_right = hop(4, sendbuf.at[0, 0, top], far1.at[0], right)
    far1_left = hop(5, sendbuf.at[0, 0, low], far1.at[1], left)
    far0_right = hop(6, sendbuf.at[3, 0], far0.at[0], right)
    far0_left = hop(7, sendbuf.at[3, 1], far0.at[1], left)
    near1_right = hop(8, sendbuf.at[1, 0], near1.at[0], right)
    near1_left = hop(9, sendbuf.at[2, 0], near1.at[1], left)
    near0_right = hop(10, sendbuf.at[5], near0.at[0], right)
    near0_left = hop(11, sendbuf.at[6], near0.at[1], left)
    cross = hop(12, sendbuf.at[4, 0], across, over)

    def work(slot):
        def one(h):
            rows = block(h, tok)
            dp = dot(vbuf[slot], cst[rows, :], NT)
            part = probs[slot, :, rows].astype(F32) * (dp - dvec[pl.ds(h, 1), :])
            dst[slot, :, rows] = part.astype(BF16)

        each(heads, one, UNROLL)
        acc[0] = dot(dst[slot], qst[...], NN) * scale
        acc[1] = dot(probs[slot], cst[...], NN)

        @pl.when(slot == 0)
        def _():
            sendbuf[0] = acc[...].astype(BF16)
            far1_right.start()
            far1_left.start()
            pair[2].start()

        @pl.when(slot == 1)
        def _():
            sendbuf[1, 1] = acc[1].astype(BF16)
            pair[1].start()
            hold[0] = acc[0]

        @pl.when(slot == 2)
        def _():
            sendbuf[2, 1] = acc[1].astype(BF16)
            pair[3].start()
            far1_right.wait_recv()
            sendbuf[1, 0, top] = (hold[0, top] + far1[0].astype(F32)).astype(BF16)
            sendbuf[1, 0, low] = hold[0, low].astype(BF16)
            near1_right.start()
            far1_left.wait_recv()
            sendbuf[2, 0, top] = acc[0, top].astype(BF16)
            sendbuf[2, 0, low] = (acc[0, low] + far1[1].astype(F32)).astype(BF16)
            near1_left.start()

        @pl.when(slot == 3)
        def _():
            sendbuf[3, 0] = acc[0].astype(BF16)
            far0_right.start()
            pair[2].wait_recv()
            sendbuf[3, 1] = (acc[1] + zin[2].astype(F32)).astype(BF16)
            far0_left.start()

        @pl.when(slot == 4)
        def _():
            sendbuf[4, 1] = acc[1].astype(BF16)
            pair[0].start()
            hold[1] = acc[0]

        @pl.when(slot == 5)
        def _():
            hold[2:4] = acc[...]

        @pl.when(slot == 6)
        def _():
            far0_right.wait_recv()
            pair[1].wait_recv()
            sendbuf[5, 0] = (hold[2] + far0[0].astype(F32)).astype(BF16)
            sendbuf[5, 1] = (hold[3] + zin[1].astype(F32)).astype(BF16)
            near0_right.start()
            far0_left.wait_recv()
            pair[3].wait_recv()
            sendbuf[6, 0] = acc[0].astype(BF16)
            sendbuf[6, 1] = (acc[1] + zin[3].astype(F32) + far0[1].astype(F32)).astype(BF16)
            near0_left.start()
            near1_right.wait_recv()
            near1_left.wait_recv()
            sendbuf[4, 0] = (hold[1] + near1[0].astype(F32) + near1[1].astype(F32)).astype(BF16)
            cross.start()

    each(8, work)
    kt = jnp.transpose(kbuf[...].reshape(8 * tok, HD))

    def finish(h):
        part = dot(kt, dst[:, :, block(h, tok)].reshape(8 * tok, tok), NN) * scale
        gq_ref[:, block(h, HD)] = jnp.transpose(part).astype(BF16)

    each(heads, finish, SPREAD)
    pair[0].wait_recv()
    gv = acc[1] + zin[0].astype(F32)
    gk = acc[0]
    near0_right.wait_recv()
    near0_left.wait_recv()
    cross.wait_recv()
    gk_ref[...] = (
        gk + near0[0, 0].astype(F32) + near0[1, 0].astype(F32) + across[...].astype(F32)
    ).astype(BF16)
    gv_ref[...] = (gv + near0[0, 1].astype(F32) + near0[1, 1].astype(F32)).astype(BF16)
    for c in (*pair.values(), far1_right, far1_left, far0_right, far0_left):
        c.wait_send()
    for c in (near1_right, near1_left, near0_right, near0_left, cross):
        c.wait_send()


def local(queries, keys, values, cotangent, positions):
    q, k, v, cot = queries[0], keys[0], values[0], cotangent[0]
    q, k, v, positions = (
        pltpu.with_memory_space_constraint(a, pltpu.HBM) for a in (q, k, v, positions)
    )
    tok, width = q.shape
    heads = width // HD
    wide = heads * tok
    count = lax.axis_size("section")
    mirrored = lax.ppermute(cot, "section", [(s, count - 1 - s) for s in range(count)])
    anywhere = pl.BlockSpec(memory_space=pl.ANY)
    vmem = pl.BlockSpec(memory_space=pltpu.VMEM)
    dma = pltpu.SemaphoreType.DMA
    out, probs, k_all, v_all, q_st, inverse = pl.pallas_call(
        functools.partial(fwd_kernel, heads, tok),
        out_shape=(
            jax.ShapeDtypeStruct((tok, width), BF16),
            jax.ShapeDtypeStruct((8, tok, wide), BF16),
            jax.ShapeDtypeStruct((8, tok, HD), BF16),
            jax.ShapeDtypeStruct((8, tok, HD), BF16),
            jax.ShapeDtypeStruct((wide, HD), BF16),
            jax.ShapeDtypeStruct((tok, width), F32),
        ),
        in_specs=[anywhere] * 4,
        out_specs=(vmem,) * 6,
        scratch_shapes=[
            pltpu.VMEM((8 * tok,), jnp.int32),
            pltpu.VMEM((8, tok, wide), F32),
            pltpu.VMEM((8, tok, tok), F32),
            pltpu.VMEM((heads, 8, tok), F32),
            pltpu.VMEM((heads, 8, tok), F32),
            dma((heads + 3,)),
            dma((8,)),
            dma((8,)),
            dma((8,)),
            dma((8,)),
        ],
        cost_estimate=pl.CostEstimate(
            flops=4 * wide * 8 * tok * HD, bytes_accessed=2**24, transcendentals=wide * 8 * tok
        ),
        compiler_params=pltpu.CompilerParams(
            collective_id=1, has_side_effects=True, vmem_limit_bytes=36 * 2**20
        ),
    )(q, k, v, positions)
    grad_q, grad_k, grad_v = pl.pallas_call(
        functools.partial(bwd_kernel, heads, tok),
        out_shape=(
            jax.ShapeDtypeStruct((tok, width), BF16),
            jax.ShapeDtypeStruct((tok, HD), BF16),
            jax.ShapeDtypeStruct((tok, HD), BF16),
        ),
        in_specs=[vmem] * 7,
        out_specs=(vmem,) * 3,
        scratch_shapes=[
            pltpu.VMEM((wide, HD), BF16),
            pltpu.VMEM((8, tok, wide), BF16),
            pltpu.VMEM((2, tok, HD), F32),
            pltpu.VMEM((4, tok, HD), F32),
            pltpu.VMEM((heads, tok), F32),
            pltpu.VMEM((7, 2, tok, HD), BF16),
            pltpu.VMEM((4, tok, HD), BF16),
            pltpu.VMEM((2, tok // 2, HD), BF16),
            pltpu.VMEM((2, tok, HD), BF16),
            pltpu.VMEM((2, tok, HD), BF16),
            pltpu.VMEM((2, 2, tok, HD), BF16),
            pltpu.VMEM((tok, HD), BF16),
            dma((13,)),
            dma((13,)),
        ],
        cost_estimate=pl.CostEstimate(
            flops=8 * wide * 8 * tok * HD, bytes_accessed=2**24, transcendentals=0
        ),
        compiler_params=pltpu.CompilerParams(
            collective_id=2, has_side_effects=True, vmem_limit_bytes=36 * 2**20
        ),
    )(mirrored, probs, k_all, v_all, q_st, out, inverse)
    return (out[None], grad_q[None], grad_k[None], grad_v[None])


def solution(mesh):
    split = P("section", "seq", "tensor")
    return jax.shard_map(
        local,
        mesh=mesh,
        in_specs=(split, split, split, split, P()),
        out_specs=(split, split, split, split),
        check_vma=False,
    )
```

```python
import functools
import math

import jax
import jax.numpy as jnp
from jax import lax
from jax.experimental import pallas as pl
from jax.experimental.pallas import tpu as pltpu
from jax.sharding import PartitionSpec as P

HD = 128
MESH = pl.DeviceIdType.MESH
NT = (((1,), (1,)), ((), ()))
NN = (((1,), (0,)), ((), ()))
F32 = jnp.float32
BF16 = jnp.bfloat16
UNROLL = 8
SPREAD = 8
WEIGH = 1


def dot(a, b, dims):
    return lax.dot_general(a, b, dims, preferred_element_type=F32)


def place():
    return tuple(lax.axis_index(a) for a in ("section", "tensor", "seq"))


ORDER = ((1, 2), (1, 1), (1, 3), (0, 2), (1, 0), (0, 1), (0, 3), (0, 0))
OWN = 7


def peer(dz, dx):
    section, tensor, seq = place()
    z, x = seq // 4, seq % 4
    return (section, tensor, ((z + dz) % 2) * 4 + (x + dx) % 4)


def greet(devices):
    barrier = pltpu.get_barrier_semaphore()
    for device in devices:
        pl.semaphore_signal(barrier, inc=1, device_id=device, device_id_type=MESH)
    pl.semaphore_wait(barrier, len(devices))


def remote(src, dst, send, recv, device):
    return pltpu.make_async_remote_copy(
        src_ref=src, dst_ref=dst, send_sem=send, recv_sem=recv, device_id=device, device_id_type=MESH
    )


def each(count, body, unroll=1):
    if unroll >= count:
        for j in range(count):
            body(j)
        return

    def step(i, carry):
        for j in range(unroll):
            body(i * unroll + j)
        return carry

    lax.fori_loop(0, count // unroll, step, 0)


def block(index, size):
    return pl.ds(index * size if isinstance(index, int) else pl.multiple_of(index * size, size), size)


def fwd_kernel(
    heads, tok, q_hbm, k_hbm, v_hbm, pos_hbm, o_ref, probs, kbuf, vbuf, qst, inv_ref,
    pos, scores, bias, top, total, lsem, ksend, krecv, vsend, vrecv,
):
    loads = [
        pltpu.make_async_copy(q_hbm.at[:, pl.ds(h * HD, HD)], qst.at[pl.ds(h * tok, tok), :], lsem.at[h])
        for h in range(heads)
    ]
    loads.append(pltpu.make_async_copy(k_hbm, kbuf.at[OWN], lsem.at[heads]))
    loads.append(pltpu.make_async_copy(v_hbm, vbuf.at[OWN], lsem.at[heads + 1]))
    loads.append(pltpu.make_async_copy(pos_hbm, pos, lsem.at[heads + 2]))
    for c in loads:
        c.start()
    greet([peer(*ORDER[slot]) for slot in range(OWN)])
    sends = []
    for src, buf, send, recv in ((k_hbm, kbuf, ksend, krecv), (v_hbm, vbuf, vsend, vrecv)):
        for slot in range(OWN):
            dz, dx = ORDER[slot]
            back = ORDER.index((dz, (4 - dx) % 4))
            sends.append(remote(src, buf.at[back], send.at[slot], recv.at[back], peer(dz, dx)))
    for c in sends:
        c.start()
    for c in loads:
        c.wait()

    def pos_row(device):
        return pos[block(device, tok)].reshape(1, tok).astype(F32)

    rows = [pos_row(peer(dz, dx)[2]) for dz, dx in ORDER]
    k_cols = jnp.transpose(jnp.concatenate(rows, axis=0))
    for slot in range(8):
        bias[slot] = jnp.where(k_cols[:, slot : slot + 1] <= rows[OWN], 0.0, -1e30)
    top[...] = jnp.full_like(top, -1e30)
    total[...] = jnp.zeros_like(total)
    factor = HD**-0.5 * math.log2(math.e)

    def score(i):
        slot = OWN - i

        @pl.when(i > 0)
        def _():
            remote(kbuf.at[slot], kbuf.at[slot], ksend.at[slot], krecv.at[slot], peer(0, 1)).wait_recv()

        def one(h):
            columns = block(h, tok)
            part = dot(kbuf[slot], qst[columns, :], NT) * factor + bias[slot]
            scores[slot, :, columns] = part
            top[h] = jnp.maximum(top[h], jnp.max(part.reshape(tok // 8, 8, tok), axis=0))

        each(heads, one, UNROLL)

    each(8, score)

    def weigh(h):
        columns = block(h, tok)
        peak = jnp.max(top[h], axis=0, keepdims=True)

        def one(slot):
            raw = jnp.exp2(scores[slot, :, columns] - peak)
            total[h] += jnp.sum(raw.reshape(tok // 8, 8, tok), axis=0)
            probs[slot, :, columns] = raw.astype(BF16)

        each(8, one, UNROLL)

    each(heads, weigh, WEIGH)
    for slot in range(OWN):
        remote(vbuf.at[slot], vbuf.at[slot], vsend.at[slot], vrecv.at[slot], peer(0, 1)).wait_recv()
    vt = jnp.transpose(vbuf[...].reshape(8 * tok, HD))

    def mix(h):
        inv = jnp.broadcast_to(1.0 / jnp.sum(total[h], axis=0, keepdims=True), (HD, tok))
        mixed = dot(vt, probs[:, :, block(h, tok)].reshape(8 * tok, tok), NN)
        o_ref[:, block(h, HD)] = jnp.transpose(mixed * inv).astype(BF16)
        inv_ref[:, block(h, HD)] = jnp.transpose(inv)

    each(heads, mix, SPREAD)
    for c in sends:
        c.wait_send()


def bwd_kernel(
    heads, tok, cot_ref, probs, kbuf, vbuf, qst, o_ref, inv_ref, done_ref, gq_ref, gk_ref, gv_ref,
    cst, dst, acc, hold, dvec, sendbuf, zin, far1, far0, near1, near0, across, ssem, rsem,
):
    scale = HD**-0.5
    right, left, over = peer(0, 1), peer(0, 3), peer(1, 0)
    greet([right, left, over])

    def prepare(h):
        columns = block(h, HD)
        cot = cot_ref[:, columns].astype(F32) * inv_ref[:, columns]
        drop = jnp.transpose(cot * o_ref[:, columns].astype(F32))
        dvec[pl.ds(h, 1), :] = jnp.sum(drop, axis=0, keepdims=True)
        cst[block(h, tok), :] = cot.astype(BF16)

    each(heads, prepare, SPREAD)

    def hop(number, src, dst_ref, device):
        return remote(src, dst_ref, ssem.at[number], rsem.at[number], device)

    top, low = pl.ds(0, tok // 2), pl.ds(tok // 2, tok // 2)
    pair = {dx: hop(dx, sendbuf.at[ORDER.index((1, dx)), 1], zin.at[dx], over) for dx in range(4)}
    far1_right = hop(4, sendbuf.at[0, 0, top], far1.at[0], right)
    far1_left = hop(5, sendbuf.at[0, 0, low], far1.at[1], left)
    far0_right = hop(6, sendbuf.at[3, 0], far0.at[0], right)
    far0_left = hop(7, sendbuf.at[3, 1], far0.at[1], left)
    near1_right = hop(8, sendbuf.at[1, 0], near1.at[0], right)
    near1_left = hop(9, sendbuf.at[2, 0], near1.at[1], left)
    near0_right = [hop(10 + i, sendbuf.at[5, i], near0.at[0, i], right) for i in range(2)]
    near0_left = [hop(12 + i, sendbuf.at[6, i], near0.at[1, i], left) for i in range(2)]
    cross = hop(14, sendbuf.at[4, 0], across, over)

    def work(slot):
        def one(h):
            rows = block(h, tok)
            dp = dot(vbuf[slot], cst[rows, :], NT)
            part = probs[slot, :, rows].astype(F32) * (dp - dvec[pl.ds(h, 1), :])
            dst[slot, :, rows] = part.astype(BF16)

        each(heads, one, UNROLL)
        acc[0] = dot(dst[slot], qst[...], NN) * scale
        acc[1] = dot(probs[slot], cst[...], NN)

        @pl.when(slot == 0)
        def _():
            sendbuf[0] = acc[...].astype(BF16)
            far1_right.start()
            far1_left.start()
            pair[2].start()

        @pl.when(slot == 1)
        def _():
            sendbuf[1, 1] = acc[1].astype(BF16)
            pair[1].start()
            hold[0] = acc[0]

        @pl.when(slot == 2)
        def _():
            sendbuf[2, 1] = acc[1].astype(BF16)
            pair[3].start()
            far1_right.wait_recv()
            sendbuf[1, 0, top] = (hold[0, top] + far1[0].astype(F32)).astype(BF16)
            sendbuf[1, 0, low] = hold[0, low].astype(BF16)
            near1_right.start()
            far1_left.wait_recv()
            sendbuf[2, 0, top] = acc[0, top].astype(BF16)
            sendbuf[2, 0, low] = (acc[0, low] + far1[1].astype(F32)).astype(BF16)
            near1_left.start()

        @pl.when(slot == 3)
        def _():
            sendbuf[3, 0] = acc[0].astype(BF16)
            far0_right.start()
            pair[2].wait_recv()
            sendbuf[3, 1] = (acc[1] + zin[2].astype(F32)).astype(BF16)
            far0_left.start()

        @pl.when(slot == 4)
        def _():
            sendbuf[4, 1] = acc[1].astype(BF16)
            pair[0].start()
            hold[1] = acc[0]

        @pl.when(slot == 5)
        def _():
            hold[2] = acc[0]
            pair[1].wait_recv()
            sendbuf[5, 1] = (acc[1] + zin[1].astype(F32)).astype(BF16)
            near0_right[1].start()

        @pl.when(slot == 6)
        def _():
            sendbuf[6, 0] = acc[0].astype(BF16)
            near0_left[0].start()
            far0_right.wait_recv()
            sendbuf[5, 0] = (hold[2] + far0[0].astype(F32)).astype(BF16)
            near0_right[0].start()
            pair[3].wait_recv()
            far0_left.wait_recv()
            sendbuf[6, 1] = (acc[1] + zin[3].astype(F32) + far0[1].astype(F32)).astype(BF16)
            near0_left[1].start()
            near1_right.wait_recv()
            near1_left.wait_recv()
            sendbuf[4, 0] = (hold[1] + near1[0].astype(F32) + near1[1].astype(F32)).astype(BF16)
            cross.start()

    each(8, work, 8)
    kt = jnp.transpose(kbuf[...].reshape(8 * tok, HD))

    def finish(h):
        part = dot(kt, dst[:, :, block(h, tok)].reshape(8 * tok, tok), NN) * scale
        gq_ref[:, block(h, HD)] = jnp.transpose(part).astype(BF16)

    each(heads, finish, SPREAD)
    pair[0].wait_recv()
    gv = acc[1] + zin[0].astype(F32)
    gk = acc[0]
    for c in (*near0_right, *near0_left, cross):
        c.wait_recv()
    gk_ref[...] = (
        gk + near0[0, 0].astype(F32) + near0[1, 0].astype(F32) + across[...].astype(F32)
    ).astype(BF16)
    gv_ref[...] = (gv + near0[0, 1].astype(F32) + near0[1, 1].astype(F32)).astype(BF16)
    for c in (*pair.values(), far1_right, far1_left, far0_right, far0_left):
        c.wait_send()
    for c in (near1_right, near1_left, *near0_right, *near0_left, cross):
        c.wait_send()


def keep_kernel(o_ref, o_hbm, done_ref, sem):
    copy = pltpu.make_async_copy(o_ref, o_hbm, sem)
    copy.start()
    done_ref[...] = jnp.zeros_like(done_ref)
    copy.wait()


def local(queries, keys, values, cotangent, positions):
    q, k, v, cot = queries[0], keys[0], values[0], cotangent[0]
    q, k, v, positions = (
        pltpu.with_memory_space_constraint(a, pltpu.HBM) for a in (q, k, v, positions)
    )
    tok, width = q.shape
    heads = width // HD
    wide = heads * tok
    count = lax.axis_size("section")
    mirrored = lax.ppermute(cot, "section", [(s, count - 1 - s) for s in range(count)])
    anywhere = pl.BlockSpec(memory_space=pl.ANY)
    vmem = pl.BlockSpec(memory_space=pltpu.VMEM)
    dma = pltpu.SemaphoreType.DMA
    out, probs, k_all, v_all, q_st, inverse = pl.pallas_call(
        functools.partial(fwd_kernel, heads, tok),
        out_shape=(
            jax.ShapeDtypeStruct((tok, width), BF16),
            jax.ShapeDtypeStruct((8, tok, wide), BF16),
            jax.ShapeDtypeStruct((8, tok, HD), BF16),
            jax.ShapeDtypeStruct((8, tok, HD), BF16),
            jax.ShapeDtypeStruct((wide, HD), BF16),
            jax.ShapeDtypeStruct((tok, width), F32),
        ),
        in_specs=[anywhere] * 4,
        out_specs=(vmem,) * 6,
        scratch_shapes=[
            pltpu.VMEM((8 * tok,), jnp.int32),
            pltpu.VMEM((8, tok, wide), F32),
            pltpu.VMEM((8, tok, tok), F32),
            pltpu.VMEM((heads, 8, tok), F32),
            pltpu.VMEM((heads, 8, tok), F32),
            dma((heads + 3,)),
            dma((8,)),
            dma((8,)),
            dma((8,)),
            dma((8,)),
        ],
        cost_estimate=pl.CostEstimate(
            flops=4 * wide * 8 * tok * HD, bytes_accessed=2**24, transcendentals=wide * 8 * tok
        ),
        compiler_params=pltpu.CompilerParams(
            collective_id=1, has_side_effects=True, vmem_limit_bytes=36 * 2**20
        ),
    )(q, k, v, positions)
    kept, done = pl.pallas_call(
        keep_kernel,
        out_shape=(jax.ShapeDtypeStruct((tok, width), BF16), jax.ShapeDtypeStruct((8, HD), F32)),
        in_specs=[vmem],
        out_specs=(pl.BlockSpec(memory_space=pltpu.HBM), vmem),
        scratch_shapes=[dma],
        compiler_params=pltpu.CompilerParams(vmem_limit_bytes=2**20),
    )(out)
    grad_q, grad_k, grad_v = pl.pallas_call(
        functools.partial(bwd_kernel, heads, tok),
        out_shape=(
            jax.ShapeDtypeStruct((tok, width), BF16),
            jax.ShapeDtypeStruct((tok, HD), BF16),
            jax.ShapeDtypeStruct((tok, HD), BF16),
        ),
        in_specs=[vmem] * 8,
        out_specs=(vmem,) * 3,
        scratch_shapes=[
            pltpu.VMEM((wide, HD), BF16),
            pltpu.VMEM((8, tok, wide), BF16),
            pltpu.VMEM((2, tok, HD), F32),
            pltpu.VMEM((3, tok, HD), F32),
            pltpu.VMEM((heads, tok), F32),
            pltpu.VMEM((7, 2, tok, HD), BF16),
            pltpu.VMEM((4, tok, HD), BF16),
            pltpu.VMEM((2, tok // 2, HD), BF16),
            pltpu.VMEM((2, tok, HD), BF16),
            pltpu.VMEM((2, tok, HD), BF16),
            pltpu.VMEM((2, 2, tok, HD), BF16),
            pltpu.VMEM((tok, HD), BF16),
            dma((15,)),
            dma((15,)),
        ],
        cost_estimate=pl.CostEstimate(
            flops=8 * wide * 8 * tok * HD, bytes_accessed=2**24, transcendentals=0
        ),
        compiler_params=pltpu.CompilerParams(
            collective_id=2, has_side_effects=True, vmem_limit_bytes=36 * 2**20
        ),
    )(mirrored, probs, k_all, v_all, q_st, out, inverse, done)
    return (kept[None], grad_q[None], grad_k[None], grad_v[None])


def solution(mesh):
    split = P("section", "seq", "tensor")
    return jax.shard_map(
        local,
        mesh=mesh,
        in_specs=(split, split, split, split, P()),
        out_specs=(split, split, split, split),
        check_vma=False,
    )
```

```python
import functools
import math

import jax
import jax.numpy as jnp
from jax import lax
from jax.experimental import pallas as pl
from jax.experimental.pallas import tpu as pltpu
from jax.sharding import PartitionSpec as P

HD = 128
MESH = pl.DeviceIdType.MESH
NT = (((1,), (1,)), ((), ()))
NN = (((1,), (0,)), ((), ()))
F32 = jnp.float32
BF16 = jnp.bfloat16
UNROLL = 8
SPREAD = 8
WEIGH = 1


def dot(a, b, dims):
    return lax.dot_general(a, b, dims, preferred_element_type=F32)


def place():
    return tuple(lax.axis_index(a) for a in ("section", "tensor", "seq"))


ORDER = ((1, 2), (1, 1), (1, 3), (0, 2), (1, 0), (0, 1), (0, 3), (0, 0))
OWN = 7


def peer(dz, dx):
    section, tensor, seq = place()
    z, x = seq // 4, seq % 4
    return (section, tensor, ((z + dz) % 2) * 4 + (x + dx) % 4)


def greet(devices):
    barrier = pltpu.get_barrier_semaphore()
    for device in devices:
        pl.semaphore_signal(barrier, inc=1, device_id=device, device_id_type=MESH)
    pl.semaphore_wait(barrier, len(devices))


def remote(src, dst, send, recv, device):
    return pltpu.make_async_remote_copy(
        src_ref=src, dst_ref=dst, send_sem=send, recv_sem=recv, device_id=device, device_id_type=MESH
    )


def each(count, body, unroll=1):
    if unroll >= count:
        for j in range(count):
            body(j)
        return

    def step(i, carry):
        for j in range(unroll):
            body(i * unroll + j)
        return carry

    lax.fori_loop(0, count // unroll, step, 0)


def block(index, size):
    return pl.ds(index * size if isinstance(index, int) else pl.multiple_of(index * size, size), size)


def fwd_kernel(
    heads, tok, q_hbm, k_hbm, v_hbm, pos_hbm, o_ref, probs, kbuf, vbuf, qst, inv_ref,
    pos, scores, bias, top, total, lsem, ksend, krecv, vsend, vrecv,
):
    loads = [
        pltpu.make_async_copy(q_hbm.at[:, pl.ds(h * HD, HD)], qst.at[pl.ds(h * tok, tok), :], lsem.at[h])
        for h in range(heads)
    ]
    loads.append(pltpu.make_async_copy(k_hbm, kbuf.at[OWN], lsem.at[heads]))
    loads.append(pltpu.make_async_copy(v_hbm, vbuf.at[OWN], lsem.at[heads + 1]))
    loads.append(pltpu.make_async_copy(pos_hbm, pos, lsem.at[heads + 2]))
    for c in loads:
        c.start()
    greet([peer(*ORDER[slot]) for slot in range(OWN)])
    sends = []
    for src, buf, send, recv in ((k_hbm, kbuf, ksend, krecv), (v_hbm, vbuf, vsend, vrecv)):
        for slot in range(OWN):
            dz, dx = ORDER[slot]
            back = ORDER.index((dz, (4 - dx) % 4))
            sends.append(remote(src, buf.at[back], send.at[slot], recv.at[back], peer(dz, dx)))
    for c in sends:
        c.start()
    for c in loads:
        c.wait()

    def pos_row(device):
        return pos[block(device, tok)].reshape(1, tok).astype(F32)

    rows = [pos_row(peer(dz, dx)[2]) for dz, dx in ORDER]
    k_cols = jnp.transpose(jnp.concatenate(rows, axis=0))
    for slot in range(8):
        bias[slot] = jnp.where(k_cols[:, slot : slot + 1] <= rows[OWN], 0.0, -1e30)
    top[...] = jnp.full_like(top, -1e30)
    total[...] = jnp.zeros_like(total)
    factor = HD**-0.5 * math.log2(math.e)

    def score(i):
        slot = OWN - i

        @pl.when(i > 0)
        def _():
            remote(kbuf.at[slot], kbuf.at[slot], ksend.at[slot], krecv.at[slot], peer(0, 1)).wait_recv()

        def one(h):
            columns = block(h, tok)
            part = dot(kbuf[slot], qst[columns, :], NT) * factor + bias[slot]
            scores[slot, :, columns] = part
            top[h] = jnp.maximum(top[h], jnp.max(part.reshape(tok // 8, 8, tok), axis=0))

        each(heads, one, UNROLL)

    each(8, score)

    def weigh(h):
        columns = block(h, tok)
        peak = jnp.max(top[h], axis=0, keepdims=True)

        def one(slot):
            raw = jnp.exp2(scores[slot, :, columns] - peak)
            total[h] += jnp.sum(raw.reshape(tok // 8, 8, tok), axis=0)
            probs[slot, :, columns] = raw.astype(BF16)

        each(8, one, UNROLL)

    each(heads, weigh, WEIGH)
    for slot in range(OWN):
        remote(vbuf.at[slot], vbuf.at[slot], vsend.at[slot], vrecv.at[slot], peer(0, 1)).wait_recv()
    vt = jnp.transpose(vbuf[...].reshape(8 * tok, HD))

    def mix(h):
        inv = jnp.broadcast_to(1.0 / jnp.sum(total[h], axis=0, keepdims=True), (HD, tok))
        mixed = dot(vt, probs[:, :, block(h, tok)].reshape(8 * tok, tok), NN)
        o_ref[:, block(h, HD)] = jnp.transpose(mixed * inv).astype(BF16)
        inv_ref[:, block(h, HD)] = jnp.transpose(inv)

    each(heads, mix, SPREAD)
    for c in sends:
        c.wait_send()


def bwd_kernel(
    heads, tok, cot_ref, probs, kbuf, vbuf, qst, o_ref, inv_ref, done_ref, gq_ref, gk_ref, gv_ref,
    cst, dst, acc, hold, dvec, sendbuf, zin, far1, far0, near1, near0, across, ssem, rsem,
):
    scale = HD**-0.5
    right, left, over = peer(0, 1), peer(0, 3), peer(1, 0)
    greet([right, left, over])

    def prepare(h):
        columns = block(h, HD)
        cot = cot_ref[:, columns].astype(F32) * inv_ref[:, columns]
        drop = jnp.transpose(cot * o_ref[:, columns].astype(F32))
        dvec[pl.ds(h, 1), :] = jnp.sum(drop, axis=0, keepdims=True)
        cst[block(h, tok), :] = cot.astype(BF16)

    each(heads, prepare, SPREAD)

    def hop(number, src, dst_ref, device):
        return remote(src, dst_ref, ssem.at[number], rsem.at[number], device)

    top, low = pl.ds(0, tok // 2), pl.ds(tok // 2, tok // 2)
    pair = {dx: hop(dx, sendbuf.at[ORDER.index((1, dx)), 1], zin.at[dx], over) for dx in range(4)}
    far1_right = hop(4, sendbuf.at[0, 0, top], far1.at[0], right)
    far1_left = hop(5, sendbuf.at[0, 0, low], far1.at[1], left)
    far0_right = hop(6, sendbuf.at[3, 0], far0.at[0], right)
    far0_left = hop(7, sendbuf.at[3, 1], far0.at[1], left)
    near1_right = hop(8, sendbuf.at[1, 0], near1.at[0], right)
    near1_left = hop(9, sendbuf.at[2, 0], near1.at[1], left)
    near0_right = [hop(10 + i, sendbuf.at[5, i], near0.at[0, i], right) for i in range(2)]
    near0_left = [hop(12 + i, sendbuf.at[6, i], near0.at[1, i], left) for i in range(2)]
    cross = hop(14, sendbuf.at[4, 0], across, over)

    def work(slot):
        def one(h):
            rows = block(h, tok)
            dp = dot(vbuf[slot], cst[rows, :], NT)
            part = probs[slot, :, rows].astype(F32) * (dp - dvec[pl.ds(h, 1), :])
            dst[slot, :, rows] = part.astype(BF16)

        each(heads, one, UNROLL)
        acc[0] = dot(dst[slot], qst[...], NN) * scale
        acc[1] = dot(probs[slot], cst[...], NN)

        @pl.when(slot == 0)
        def _():
            sendbuf[0] = acc[...].astype(BF16)
            far1_right.start()
            far1_left.start()
            pair[2].start()

        @pl.when(slot == 1)
        def _():
            sendbuf[1, 1] = acc[1].astype(BF16)
            pair[1].start()
            hold[0] = acc[0]

        @pl.when(slot == 2)
        def _():
            sendbuf[2, 1] = acc[1].astype(BF16)
            pair[3].start()
            far1_right.wait_recv()
            sendbuf[1, 0, top] = (hold[0, top] + far1[0].astype(F32)).astype(BF16)
            sendbuf[1, 0, low] = hold[0, low].astype(BF16)
            near1_right.start()
            far1_left.wait_recv()
            sendbuf[2, 0, top] = acc[0, top].astype(BF16)
            sendbuf[2, 0, low] = (acc[0, low] + far1[1].astype(F32)).astype(BF16)
            near1_left.start()

        @pl.when(slot == 3)
        def _():
            sendbuf[3, 0] = acc[0].astype(BF16)
            far0_right.start()
            pair[2].wait_recv()
            sendbuf[3, 1] = (acc[1] + zin[2].astype(F32)).astype(BF16)
            far0_left.start()

        @pl.when(slot == 4)
        def _():
            sendbuf[4, 1] = acc[1].astype(BF16)
            pair[0].start()
            hold[1] = acc[0]

        @pl.when(slot == 5)
        def _():
            hold[2] = acc[0]
            pair[1].wait_recv()
            sendbuf[5, 1] = (acc[1] + zin[1].astype(F32)).astype(BF16)
            near0_right[1].start()

        @pl.when(slot == 6)
        def _():
            sendbuf[6, 0] = acc[0].astype(BF16)
            near0_left[0].start()
            far0_right.wait_recv()
            sendbuf[5, 0] = (hold[2] + far0[0].astype(F32)).astype(BF16)
            near0_right[0].start()
            pair[3].wait_recv()
            far0_left.wait_recv()
            sendbuf[6, 1] = (acc[1] + zin[3].astype(F32) + far0[1].astype(F32)).astype(BF16)
            near0_left[1].start()
            near1_right.wait_recv()
            near1_left.wait_recv()
            sendbuf[4, 0] = (hold[1] + near1[0].astype(F32) + near1[1].astype(F32)).astype(BF16)
            cross.start()

    each(8, work, 8)
    kt = jnp.transpose(kbuf[...].reshape(8 * tok, HD))

    def finish(h):
        part = dot(kt, dst[:, :, block(h, tok)].reshape(8 * tok, tok), NN) * scale
        gq_ref[:, block(h, HD)] = jnp.transpose(part).astype(BF16)

    each(heads, finish, SPREAD)
    pair[0].wait_recv()
    gv = acc[1] + zin[0].astype(F32)
    gk = acc[0]
    for c in (*near0_right, *near0_left, cross):
        c.wait_recv()
    gk_ref[...] = (
        gk + near0[0, 0].astype(F32) + near0[1, 0].astype(F32) + across[...].astype(F32)
    ).astype(BF16)
    gv_ref[...] = (gv + near0[0, 1].astype(F32) + near0[1, 1].astype(F32)).astype(BF16)
    for c in (*pair.values(), far1_right, far1_left, far0_right, far0_left):
        c.wait_send()
    for c in (near1_right, near1_left, *near0_right, *near0_left, cross):
        c.wait_send()


def keep_kernel(o_ref, o_hbm, done_ref, sem):
    copy = pltpu.make_async_copy(o_ref, o_hbm, sem)
    copy.start()
    done_ref[...] = jnp.zeros_like(done_ref)
    copy.wait()


def place_kernel(*refs):
    count = len(refs) // 2
    copies = [pltpu.make_async_copy(refs[i], refs[count + i], refs[-1].at[i]) for i in range(count)]
    for c in copies:
        c.start()
    for c in copies:
        c.wait()


def local(queries, keys, values, cotangent, positions):
    q, k, v, cot = queries[0], keys[0], values[0], cotangent[0]
    q, k, v, positions = (
        pltpu.with_memory_space_constraint(a, pltpu.HBM) for a in (q, k, v, positions)
    )
    tok, width = q.shape
    heads = width // HD
    wide = heads * tok
    count = lax.axis_size("section")
    mirrored = lax.ppermute(cot, "section", [(s, count - 1 - s) for s in range(count)])
    anywhere = pl.BlockSpec(memory_space=pl.ANY)
    vmem = pl.BlockSpec(memory_space=pltpu.VMEM)
    dma = pltpu.SemaphoreType.DMA
    out, probs, k_all, v_all, q_st, inverse = pl.pallas_call(
        functools.partial(fwd_kernel, heads, tok),
        out_shape=(
            jax.ShapeDtypeStruct((tok, width), BF16),
            jax.ShapeDtypeStruct((8, tok, wide), BF16),
            jax.ShapeDtypeStruct((8, tok, HD), BF16),
            jax.ShapeDtypeStruct((8, tok, HD), BF16),
            jax.ShapeDtypeStruct((wide, HD), BF16),
            jax.ShapeDtypeStruct((tok, width), F32),
        ),
        in_specs=[anywhere] * 4,
        out_specs=(vmem,) * 6,
        scratch_shapes=[
            pltpu.VMEM((8 * tok,), jnp.int32),
            pltpu.VMEM((8, tok, wide), F32),
            pltpu.VMEM((8, tok, tok), F32),
            pltpu.VMEM((heads, 8, tok), F32),
            pltpu.VMEM((heads, 8, tok), F32),
            dma((heads + 3,)),
            dma((8,)),
            dma((8,)),
            dma((8,)),
            dma((8,)),
        ],
        cost_estimate=pl.CostEstimate(
            flops=4 * wide * 8 * tok * HD, bytes_accessed=2**24, transcendentals=wide * 8 * tok
        ),
        compiler_params=pltpu.CompilerParams(
            collective_id=1, has_side_effects=True, vmem_limit_bytes=36 * 2**20
        ),
    )(q, k, v, positions)
    kept, done = pl.pallas_call(
        keep_kernel,
        out_shape=(jax.ShapeDtypeStruct((tok, width), BF16), jax.ShapeDtypeStruct((8, HD), F32)),
        in_specs=[vmem],
        out_specs=(pl.BlockSpec(memory_space=pltpu.HBM), vmem),
        scratch_shapes=[dma],
        compiler_params=pltpu.CompilerParams(vmem_limit_bytes=2**20),
    )(out)
    grad_q, grad_k, grad_v = pl.pallas_call(
        functools.partial(bwd_kernel, heads, tok),
        out_shape=(
            jax.ShapeDtypeStruct((tok, width), BF16),
            jax.ShapeDtypeStruct((tok, HD), BF16),
            jax.ShapeDtypeStruct((tok, HD), BF16),
        ),
        in_specs=[vmem] * 8,
        out_specs=(vmem,) * 3,
        scratch_shapes=[
            pltpu.VMEM((wide, HD), BF16),
            pltpu.VMEM((8, tok, wide), BF16),
            pltpu.VMEM((2, tok, HD), F32),
            pltpu.VMEM((3, tok, HD), F32),
            pltpu.VMEM((heads, tok), F32),
            pltpu.VMEM((7, 2, tok, HD), BF16),
            pltpu.VMEM((4, tok, HD), BF16),
            pltpu.VMEM((2, tok // 2, HD), BF16),
            pltpu.VMEM((2, tok, HD), BF16),
            pltpu.VMEM((2, tok, HD), BF16),
            pltpu.VMEM((2, 2, tok, HD), BF16),
            pltpu.VMEM((tok, HD), BF16),
            dma((15,)),
            dma((15,)),
        ],
        cost_estimate=pl.CostEstimate(
            flops=8 * wide * 8 * tok * HD, bytes_accessed=2**24, transcendentals=0
        ),
        compiler_params=pltpu.CompilerParams(
            collective_id=2, has_side_effects=True, vmem_limit_bytes=36 * 2**20
        ),
    )(mirrored, probs, k_all, v_all, q_st, out, inverse, done)
    grads = (grad_q, grad_k, grad_v)
    grad_q, grad_k, grad_v = pl.pallas_call(
        place_kernel,
        out_shape=tuple(jax.ShapeDtypeStruct(g.shape, g.dtype) for g in grads),
        in_specs=[vmem] * 3,
        out_specs=(pl.BlockSpec(memory_space=pltpu.HBM),) * 3,
        scratch_shapes=[dma((3,))],
        compiler_params=pltpu.CompilerParams(vmem_limit_bytes=2**20),
    )(*grads)
    return (kept[None], grad_q[None], grad_k[None], grad_v[None])


def solution(mesh):
    split = P("section", "seq", "tensor")
    return jax.shard_map(
        local,
        mesh=mesh,
        in_specs=(split, split, split, split, P()),
        out_specs=(split, split, split, split),
        check_vma=False,
    )
```
